256 devices in a mesh: seq: 64 (over y, z, core), col: 4 (over x).
Axes of the slice: x: 4, y: 4, z: 8, core: 2. Of those that a mesh axis runs over, the one named last changes fastest.
Arguments:
- activations: bfloat16 [65536, 3584], P('seq', 'col'), may hold values from -60 to 60
- start_basis: bfloat16 [3584, 512], P('col'), may hold values from -6 to 6
- gradient: bfloat16 [3584, 3584], P(None, ('seq', 'col')), may hold values from -12 to 12
Outputs:
- projected: bfloat16 [3584, 3584], P(None, ('seq', 'col'))
The draws below stay inside these ranges and needn't reach their ends.
All inputs are finite; a program needn't handle non-finite values.
Results may differ from the reference program's by a relative error of at most 0.019.
Values may be sent and summed in bfloat16 or wider, within the bound.
A program may use at most 64 MiB of HBM per device.

```python
import jax
import jax.numpy as jnp
from jax import lax

D = 3584
DOUT = 3584
K = 512
ITERS = 2
TOKENS = 65536
N_COL = 4


def feature_scales(key):
    return jnp.exp(jax.random.uniform(jax.random.fold_in(key, 7), (D, 1), jnp.float32, jnp.log(0.4), jnp.log(2.5)))


def draw_activations(key, part):
    noise_key = jax.random.fold_in(key, 11)
    row_key = jax.random.fold_in(key, 13)
    values = jnp.clip(jax.random.normal(noise_key, (TOKENS, D), jnp.float32), -4.0, 4.0)
    row_scale = jnp.exp(jax.random.uniform(row_key, (TOKENS, 1), jnp.float32, jnp.log(0.5), jnp.log(2.0)))
    token_ramp = jnp.exp(0.55 * jnp.arange(TOKENS, dtype=jnp.float32)[:, None] / TOKENS)
    scaled = values * row_scale * token_ramp * feature_scales(key).T
    return jnp.clip(scaled, -60.0, 60.0).astype(jnp.bfloat16)


def draw_gradient(key, part):
    noise_key = jax.random.fold_in(key, 19)
    values = jnp.clip(jax.random.normal(noise_key, (D, DOUT), jnp.float32), -4.0, 4.0)
    return jnp.clip(values * feature_scales(key), -12.0, 12.0).astype(jnp.bfloat16)


def levels(rng, extent, shards, smallest, top_value):
    level = 1.0
    for position, parts in shards:
        draws = jax.random.uniform(jax.random.fold_in(jax.random.fold_in(rng, 6), position), (parts,), jnp.float32, smallest / len(shards), top_value / len(shards))
        level = level * jnp.repeat(jnp.exp(draws), extent[position] // parts).reshape((-1,) + (1,) * (len(extent) - 1 - position))
    return level


def scatter_about(rng, shape, width, limit, shards=(), held_as=jnp.bfloat16):
    array = width * jax.random.normal(rng, shape, jnp.float32)
    if shards:
        array = array * levels(rng, shape, shards, -0.22, 0.18)
    return jnp.clip(array, -limit, limit).astype(held_as)


def setup_inputs(seed: int = 0) -> dict:
    seeds = jax.random.split(jax.random.key(seed), 4)
    activations = draw_activations(jax.random.fold_in(seeds[3], 71), 0)
    start_basis = scatter_about(seeds[1], (D, K), 1.0, 6.0, ((0, 4),))
    gradient = draw_gradient(jax.random.fold_in(seeds[3], 71), 0)
    return {"activations": activations, "start_basis": start_basis, "gradient": gradient}


def contract_rows(left, right):
    return lax.dot_general(left.astype(jnp.float32), right.astype(jnp.float32), (((0,), (0,)), ((), ())), preferred_element_type=jnp.float32)

def reference(activations, start_basis, gradient):
    quarter = D // N_COL
    basis_now = start_basis
    for sweep_index in range(ITERS):
        mixed_sum = jnp.zeros((activations.shape[0], K), jnp.float32)
        for column in range(N_COL):
            partial_value = jnp.dot(activations[:, column * quarter:(column + 1) * quarter].astype(jnp.float32), basis_now[column * quarter:(column + 1) * quarter].astype(jnp.float32), preferred_element_type=jnp.float32)
            rounded = lax.optimization_barrier(partial_value.astype(jnp.bfloat16))
            mixed_sum = mixed_sum + rounded.astype(jnp.float32)
        token_mix = mixed_sum.astype(jnp.bfloat16)
        moment = contract_rows(activations, token_mix) * (1.0 / TOKENS)
        gram_sum = lax.dot_general(moment.astype(jnp.float32), moment.astype(jnp.float32), (((0,), (0,)), ((), ())), precision=lax.Precision.HIGHEST, preferred_element_type=jnp.float32)
        factor_low = jnp.linalg.cholesky(gram_sum)
        solved = jax.scipy.linalg.solve_triangular(factor_low, moment.T, lower=True)
        basis_now = solved.T.astype(jnp.bfloat16)
    coefficients = contract_rows(basis_now, gradient).astype(jnp.bfloat16)
    removed = jnp.dot(basis_now.astype(jnp.float32), coefficients.astype(jnp.float32), preferred_element_type=jnp.float32)
    return (gradient.astype(jnp.float32) - removed).astype(jnp.bfloat16)
```

```python
import functools

import jax
import jax.numpy as jnp
from jax import lax
from jax.experimental import pallas as pl
from jax.experimental.pallas import tpu as pltpu
from jax.sharding import PartitionSpec as P

MESH = pl.DeviceIdType.MESH
F32 = jnp.float32
BF16 = jnp.bfloat16
NX, NY, NZ, NC = 4, 4, 8, 2
Q = 4
W = 128
STAGES = 11


def dot(left, right):
    return jnp.dot(left, right, preferred_element_type=F32)


def dot32(left, right, dims=((1,), (0,))):
    return lax.dot_general(
        left, right, (dims, ((), ())), precision=lax.Precision.HIGHEST, preferred_element_type=F32
    )


def eliminate(groups, off):
    sub = lax.broadcasted_iota(jnp.int32, (8, 128), 0)
    lane = lax.broadcasted_iota(jnp.int32, (8, 128), 1)
    count = len(groups)
    for j in range(8 * count):
        first, r = divmod(j, 8)
        row = groups[first][r : r + 1, :]
        scaled = row * (1.0 / row[:, off + j : off + j + 1])
        for g in range(first, count):
            column = jnp.broadcast_to(groups[g][:, off + j : off + j + 1], (8, 128))
            if g == first:
                if r == 7:
                    continue
                column = jnp.where(sub > r, column, 0.0)
            groups[g] = groups[g] - column * scaled
    out = []
    for g in range(count):
        pivot = jnp.sum(jnp.where(lane == off + 8 * g + sub, groups[g], 0.0), axis=1, keepdims=True)
        out.append(groups[g] * lax.rsqrt(pivot))
    return jnp.concatenate(out, axis=0)


def inverse_factor(block):
    lane = lax.broadcasted_iota(jnp.int32, (64, 128), 1)
    row = lax.broadcasted_iota(jnp.int32, (64, 128), 0)
    top, bottom = block[:64, :], block[64:, :]
    start = jnp.where(lane < 64, top, jnp.where(lane - 64 == row, 1.0, 0.0))
    first = eliminate([start[8 * g : 8 * g + 8] for g in range(8)], 0)
    first = jnp.where(lane < 64, pltpu.roll(first, 64, 1), 0.0)
    inv1 = first[:, :64]
    upper = dot32(inv1, top)
    both = dot32(upper, upper, ((0,), (0,)))
    rest = bottom - both[64:, :]
    start = jnp.where(lane >= 64, rest, jnp.where(lane == row, 1.0, 0.0))
    cross = dot32(upper, first, ((0,), (0,)))[64:, :]
    second = eliminate([start[8 * g : 8 * g + 8] for g in range(8)], 64)
    second = jnp.where(lane < 64, second, 0.0)
    low = dot32(second[:, :64], cross)
    last = jnp.where(lane < 64, -low, pltpu.roll(second, 64, 1))
    return jnp.concatenate([first, last], axis=0)


def kernel(inv_count, a, b, grad, out, at, part, xrecv, mix, csend, chalf, crecv, ybuf, yrecv,
           zbuf, zrecv, zg, mfull, m2, mt, linv, fbf, wbuf, send, recv):
    seq, c = lax.axis_index("seq"), lax.axis_index("col")
    core, z, y = lax.rem(seq, NC), lax.rem(seq // NC, NZ), seq // (NC * NZ)

    def x_peer(d):
        return lax.rem(c + d, NX)

    def y_peer(d):
        return lax.rem(y + d, NY)

    def z_peer(d):
        return lax.rem(z + d, NZ)

    def at_x(d):
        return (seq, x_peer(d))

    def at_y(d):
        return ((y_peer(d) * NZ + z) * NC + core, c)

    def at_z(d):
        return ((y * NZ + z_peer(d)) * NC + core, c)

    at_core = ((y * NZ + z) * NC + 1 - core, c)

    barrier = pltpu.get_barrier_semaphore()
    peers = ([at_x(d) for d in range(1, NX)] + [at_y(d) for d in range(1, NY)]
             + [at_z(d) for d in range(1, NZ)] + [at_core])
    for peer in peers:
        pl.semaphore_signal(barrier, inc=1, device_id=peer, device_id_type=MESH)
    pl.semaphore_wait(barrier, len(peers))

    sent = []

    def push(i, stage, src, dst, device):
        copy = pltpu.make_async_remote_copy(
            src_ref=src, dst_ref=dst, send_sem=send.at[i, stage], recv_sem=recv.at[i, stage],
            device_id=device, device_id_type=MESH)
        copy.start()

    def arrived(i, stage, like):
        pltpu.make_async_copy(like, like, recv.at[i, stage]).wait()
        sent.append((i, stage, like))

    half = a.shape[1] // NC
    piece = half // NY

    def s1(i):
        q = i % Q
        if i < Q:
            rhs = b[:, q * W : (q + 1) * W]
        else:
            rhs = mfull[i - Q, c].reshape(a.shape[1], W)
        rows = part.shape[2]
        for d in (1, 2, 3, 0):
            p = x_peer(d)
            left = a[pl.ds(pl.multiple_of(p * rows, rows), rows), :]
            part[i, p] = dot(left, rhs).astype(BF16)
            if d:
                push(i, 0, part.at[i, p], xrecv.at[i, d - 1], at_x(d))

    def s2(i):
        arrived(i, 0, xrecv.at[i])
        total = part[i, c].astype(F32)
        for d in range(NX - 1):
            total = total + xrecv[i, d].astype(F32)
        mix[i, c] = total.astype(BF16)
        for d in (1, 2, 3):
            push(i, 1, mix.at[i, c], mix.at[i, c], at_x(d))

    def s3(i):
        arrived(i, 1, mix.at[i, pl.ds(0, NX - 1)])
        right = mix[i].reshape(a.shape[0], W)
        left = at[pl.ds(pl.multiple_of((1 - core) * half, half), half), :]
        csend[i] = (dot(left, right) * inv_count).astype(BF16)
        push(i, 2, csend.at[i], crecv.at[i], at_core)
        left = at[pl.ds(pl.multiple_of(core * half, half), half), :]
        chalf[i] = dot(left, right) * inv_count

    def s4(i):
        arrived(i, 2, crecv.at[i])
        ybuf[i] = (chalf[i] + crecv[i].astype(F32)).astype(BF16).reshape(NY, piece, W)
        for d in (1, 2, 3):
            push(i, 3, ybuf.at[i, y_peer(d)], yrecv.at[i, d - 1], at_y(d))

    def s5(i):
        arrived(i, 3, yrecv.at[i])
        total = ybuf[i, y].astype(F32)
        for d in range(NY - 1):
            total = total + yrecv[i, d].astype(F32)
        zbuf[i, : NZ - 1] = total.astype(BF16).reshape(NZ - 1, 16, W)
        zbuf[i, NZ - 1] = jnp.zeros((16, W), BF16)
        for d in range(1, NZ):
            push(i, 4, zbuf.at[i, z_peer(d)], zrecv.at[i, d - 1], at_z(d))

    def s6(i):
        arrived(i, 4, zrecv.at[i])
        total = zbuf[i, z].astype(F32)
        for d in range(NZ - 1):
            total = total + zrecv[i, d].astype(F32)
        zg[i, pl.ds(pl.multiple_of(z * 16, 16), 16), :] = total.astype(BF16)
        mine = zg.at[i, pl.ds(pl.multiple_of(z * 16, 16), 16), :]
        for d in range(1, NZ):
            push(i, 5, mine, mine, at_z(d))

    def s7(i):
        arrived(i, 5, zg.at[i, pl.ds(0, piece), :])
        src = zg.at[i, pl.ds(0, piece), :]
        dst = mfull.at[i, c, core * NY + y]
        for d in (1, 2, 3):
            push(i, 6, src, dst, at_y(d))
        for d in (1, 2, 3):
            push(i, 7, src, dst, at_x(d))
        mfull[i, c, core * NY + y] = zg[i, :piece, :]

    def s8a(i):
        arrived(i, 6, mfull.at[i, 0, pl.ds(0, NY - 1)])
        mine = mfull.at[i, c, pl.ds(core * NY, NY)]
        push(i, 8, mine, mine, at_core)

    def s8b(i):
        arrived(i, 7, mfull.at[i, 0, pl.ds(0, NX - 1)])
        for e in (1, 2, 3):
            held = mfull.at[i, x_peer(e), core * NY + y]
            for d in (1, 2, 3):
                push(i, 9, held, held, at_y(d))

    def s9a(i):
        arrived(i, 8, mfull.at[i, 0, pl.ds(0, NY)])

    def s9b(i):
        arrived(i, 9, mfull.at[i, pl.ds(0, NX - 1), pl.ds(0, NY - 1)])
        for e in (1, 2, 3):
            held = mfull.at[i, x_peer(e), pl.ds(core * NY, NY)]
            push(i, 10, held, held, at_core)

    def s10(i):
        arrived(i, 10, mfull.at[i, pl.ds(0, NX - 1), pl.ds(0, NY)])

    quarter = a.shape[1]

    def factor(i):
        sweep, q = divmod(i, Q)
        lo = q * W

        def load(x):
            rows = pl.ds(pl.multiple_of(x * quarter, quarter), quarter)
            if sweep == 0:
                block = mfull[i, x].reshape(quarter, W)
            else:
                total = jnp.zeros((quarter, W), F32)
                for k in range(q + 1):
                    total = total + dot(mfull[Q + k, x].reshape(quarter, W), fbf[q, k])
                block = total.astype(BF16)
            m2[sweep, q, rows, :] = block
            mt[sweep, pl.ds(lo, W), rows] = block.T

        pl.loop(0, NX)(load)
        gram = dot(mt[sweep, : lo + W, :], m2[sweep, q])
        if sweep:
            wbuf[pl.ds(lo, W), :] = dot(mt[sweep, lo : lo + W, :], grad[...])
        block = gram[lo:, :]
        if q:
            known = linv[sweep, :lo, :lo]
            upper = dot32(known, gram[:lo, :])
            block = block - dot32(upper, upper, ((0,), (0,)))
            cross = dot32(upper, known, ((0,), (0,)))
        inverse = inverse_factor(block)
        linv[sweep, pl.ds(lo, W), pl.ds(lo, W)] = inverse
        if q:
            low = -dot32(inverse, cross)
            linv[sweep, pl.ds(lo, W), pl.ds(0, lo)] = low
        if q < Q - 1:
            linv[sweep, pl.ds(lo, W), pl.ds(lo + W, Q * W - lo - W)] = jnp.zeros((W, Q * W - lo - W), F32)
        if sweep == 0:
            for k in range(q):
                fbf[q, k] = low[:, k * W : (k + 1) * W].T.astype(BF16)
            fbf[q, q] = inverse.T.astype(BF16)

    def finish():
        inverse = linv[1]
        coefficients = dot32(inverse, wbuf[...])
        solved = dot32(inverse, coefficients, ((0,), (0,)))
        high = solved.astype(BF16)
        low = (solved - high.astype(F32)).astype(BF16)

        def rows_of(x):
            rows = pl.ds(pl.multiple_of(x * (quarter // 2), quarter // 2), quarter // 2)
            removed = jnp.zeros((quarter // 2, grad.shape[1]), F32)
            for q in range(Q):
                block = m2[1, q, rows, :]
                removed = removed + dot(block, high[q * W : (q + 1) * W]) + dot(block, low[q * W : (q + 1) * W])
            out[rows, :] = (grad[rows, :].astype(F32) - removed).astype(BF16)

        pl.loop(0, 2 * NX)(rows_of)

    def transpose():
        for k in range(a.shape[0] // W):
            at[:, k * W : (k + 1) * W] = a[k * W : (k + 1) * W, :].T

    for sweep in range(2):
        chunks = range(sweep * Q, sweep * Q + Q)
        for i in chunks:
            s1(i)
        if sweep == 0:
            transpose()
        for stage in (s2, s3, s4, s5, s6, s7, s8a, s8b, s9a, s9b):
            for i in chunks:
                stage(i)
            if sweep and stage in (s2, s4, s6, s8a):
                k = (s2, s4, s6, s8a).index(stage)
                if k == 0:
                    for i in range(Q):
                        s10(i)
                factor(k)
    for i in range(Q, 2 * Q):
        s10(i)
        factor(i)
    finish()
    for i, stage, like in sent:
        pltpu.make_async_copy(like, like, send.at[i, stage]).wait()


def on_device(activations, start_basis, gradient):
    tokens, quarter = activations.shape
    inv_count = 1.0 / (tokens * lax.axis_size("seq"))
    n = 2 * Q
    half = quarter // NC
    piece = half // NY
    rows = tokens // NX
    vmem = pltpu.VMEM
    features = NX * quarter
    return pl.pallas_call(
        functools.partial(kernel, inv_count),
        out_shape=jax.ShapeDtypeStruct(gradient.shape, BF16),
        in_specs=[pl.BlockSpec(memory_space=pltpu.VMEM)] * 3,
        out_specs=pl.BlockSpec(memory_space=pltpu.VMEM),
        scratch_shapes=[
            vmem((quarter, tokens), BF16),
            vmem((n, NX, rows, W), BF16),
            vmem((n, NX - 1, rows, W), BF16),
            vmem((n, NX, rows, W), BF16),
            vmem((n, half, W), BF16),
            vmem((n, half, W), F32),
            vmem((n, half, W), BF16),
            vmem((n, NY, piece, W), BF16),
            vmem((n, NY - 1, piece, W), BF16),
            vmem((n, NZ, 16, W), BF16),
            vmem((n, NZ - 1, 16, W), BF16),
            vmem((n, NZ * 16, W), BF16),
            vmem((n, NX, NC * NY, piece, W), BF16),
            vmem((2, Q, features, W), BF16),
            vmem((2, Q * W, features), BF16),
            vmem((2, Q * W, Q * W), F32),
            vmem((Q, Q, W, W), BF16),
            vmem((Q * W, gradient.shape[1]), F32),
            pltpu.SemaphoreType.DMA((n, STAGES)),
            pltpu.SemaphoreType.DMA((n, STAGES)),
        ],
        compiler_params=pltpu.CompilerParams(
            collective_id=0, has_side_effects=True, vmem_limit_bytes=60 * 1024 * 1024
        ),
    )(activations, start_basis, gradient)


def solution(mesh):
    return jax.shard_map(
        on_device,
        mesh=mesh,
        in_specs=(P("seq", "col"), P("col", None), P(None, ("seq", "col"))),
        out_specs=P(None, ("seq", "col")),
        check_vma=False,
    )
```

```python
import functools

import jax
import jax.numpy as jnp
from jax import lax
from jax.experimental import pallas as pl
from jax.experimental.pallas import tpu as pltpu
from jax.sharding import PartitionSpec as P

MESH = pl.DeviceIdType.MESH
F32 = jnp.float32
BF16 = jnp.bfloat16
NX, NY, NZ, NC = 4, 4, 8, 2
Q = 4
W = 128
STAGES = 11
ORDER = (
    (0, 0), (0, 1), (0, 2), ("T", 0), (0, 3), (1, 0), (1, 1), (1, 2),
    (1, 3), (2, 0), (3, 0), (2, 1), (4, 0), (3, 1), (2, 2), (5, 0),
    (4, 1), (3, 2), (2, 3), (6, 0), (5, 1), (4, 2), (3, 3), (7, 0),
    (8, 0), (6, 1), (0, 4), (5, 2), (4, 3), (8, 1), (6, 2), (5, 3),
    (9, 0), (7, 1), (1, 4), ("F", 0), (6, 3), (8, 2), ("F", 0), (7, 2),
    (7, 3), (9, 1), (2, 4), (8, 3), ("F", 0), (9, 2), (3, 4), (0, 5),
    (0, 6), ("F", 1), (4, 4), (9, 3), ("F", 1), (5, 4), (1, 5), ("F", 1),
    (6, 4), (1, 6), (0, 7), (2, 5), ("F", 2), (7, 4), (8, 4), (3, 5),
    ("F", 2), (2, 6), (1, 7), ("F", 2), (9, 4), (4, 5), (3, 6), ("F", 3),
    (5, 5), (4, 6), (2, 7), ("F", 3), (6, 5), (5, 6), (3, 7), ("F", 3),
    (7, 5), (8, 5), (6, 6), (4, 7), ("F", 4), (8, 6), (5, 7), ("F", 4),
    (9, 5), (7, 6), (6, 7), ("F", 4), (8, 7), ("F", 5), (9, 6), (7, 7),
    ("F", 5), (9, 7), ("F", 5), ("F", 6), ("F", 6), ("F", 6), ("F", 7), ("F", 7),
    ("F", 7),
)


def dot(left, right):
    return jnp.dot(left, right, preferred_element_type=F32)


def dot32(left, right, dims=((1,), (0,))):
    return lax.dot_general(
        left, right, (dims, ((), ())), precision=lax.Precision.HIGHEST, preferred_element_type=F32
    )


def across(block, lane):
    return jnp.broadcast_to(block[:, lane : lane + 1], (8, 128))


def reciprocal(value):
    guess = pl.reciprocal(value, approx=True)
    return guess * (2.0 - value * guess)


def eliminate(groups, off):
    sub = lax.broadcasted_iota(jnp.int32, (8, 128), 0)
    groups = list(groups)
    count = len(groups)
    out = []
    for g in range(count):
        lo = off + 8 * g
        rows = [jnp.broadcast_to(groups[g][k : k + 1, :], (8, 128)) for k in range(8)]
        square = {(k, c): across(rows[k], lo + c) for k in range(8) for c in range(k, 8)}
        inverse, factor = [], {}
        for k in range(8):
            inverse.append(reciprocal(square[k, k]))
            for i in range(k + 1, 8):
                factor[i, k] = square[k, i] * inverse[k]
                for j in range(i, 8):
                    square[i, j] = square[i, j] - factor[i, k] * square[k, j]
                rows[i] = rows[i] - factor[i, k] * rows[k]
        if g + 1 < count:
            columns = [across(groups[g + 1], lo + k) for k in range(8)]
            for i in range(8):
                for k in range(i):
                    columns[i] = columns[i] - factor[i, k] * columns[k]
            for k in range(8):
                groups[g + 1] = groups[g + 1] - (columns[k] * inverse[k]) * rows[k]
        result = rows[0] * lax.rsqrt(square[0, 0])
        for k in range(1, 8):
            result = jnp.where(sub == k, rows[k] * lax.rsqrt(square[k, k]), result)
        if g + 2 < count:
            turned = result.T
            scaled = [rows[k] * lax.rsqrt(square[k, k]) for k in range(8)]
            for other in range(g + 2, count):
                columns = turned[off + 8 * other : off + 8 * other + 8, :]
                for k in range(8):
                    groups[other] = groups[other] - across(columns, k) * scaled[k]
        out.append(result)
    return jnp.concatenate(out, axis=0)


def inverse_factor(block):
    lane = lax.broadcasted_iota(jnp.int32, (64, 128), 1)
    row = lax.broadcasted_iota(jnp.int32, (64, 128), 0)
    top, bottom = block[:64, :], block[64:, :]
    start = jnp.where(lane < 64, top, jnp.where(lane - 64 == row, 1.0, 0.0))
    first = eliminate([start[8 * g : 8 * g + 8] for g in range(8)], 0)
    first = jnp.where(lane < 64, pltpu.roll(first, 64, 1), 0.0)
    yield
    inv1 = first[:, :64]
    upper = dot32(inv1, top)
    both = dot32(upper, upper, ((0,), (0,)))
    rest = bottom - both[64:, :]
    start = jnp.where(lane >= 64, rest, jnp.where(lane == row, 1.0, 0.0))
    cross = dot32(upper, first, ((0,), (0,)))[64:, :]
    second = eliminate([start[8 * g : 8 * g + 8] for g in range(8)], 64)
    second = jnp.where(lane < 64, second, 0.0)
    low = dot32(second[:, :64], cross)
    last = jnp.where(lane < 64, -low, pltpu.roll(second, 64, 1))
    return jnp.concatenate([first, last], axis=0)


def kernel(inv_count, a, b, grad, out, at, part, xrecv, mix, csend, chalf, crecv, ybuf, yrecv,
           zbuf, zrecv, zg, mfull, raw, mt, linv, fbf, wbuf, send, recv):
    seq, c = lax.axis_index("seq"), lax.axis_index("col")
    core, z, y = lax.rem(seq, NC), lax.rem(seq // NC, NZ), seq // (NC * NZ)

    def x_peer(d):
        return lax.rem(c + d, NX)

    def y_peer(d):
        return lax.rem(y + d, NY)

    def z_peer(d):
        return lax.rem(z + d, NZ)

    def at_x(d):
        return (seq, x_peer(d))

    def at_y(d):
        return ((y_peer(d) * NZ + z) * NC + core, c)

    def at_z(d):
        return ((y * NZ + z_peer(d)) * NC + core, c)

    at_core = ((y * NZ + z) * NC + 1 - core, c)

    barrier = pltpu.get_barrier_semaphore()
    peers = ([at_x(d) for d in range(1, NX)] + [at_y(d) for d in range(1, NY)]
             + [at_z(d) for d in range(1, NZ)] + [at_core])
    for peer in peers:
        pl.semaphore_signal(barrier, inc=1, device_id=peer, device_id_type=MESH)
    pl.semaphore_wait(barrier, len(peers))

    sent = []

    def push(i, stage, src, dst, device):
        copy = pltpu.make_async_remote_copy(
            src_ref=src, dst_ref=dst, send_sem=send.at[i, stage], recv_sem=recv.at[i, stage],
            device_id=device, device_id_type=MESH)
        copy.start()

    def arrived(i, stage, like):
        pltpu.make_async_copy(like, like, recv.at[i, stage]).wait()
        sent.append((i, stage, like))

    half = a.shape[1] // NC
    piece = half // NY

    def s1(i):
        q = i % Q
        if i >= Q:
            arrived(i - Q, 8, mfull.at[i - Q, 0, pl.ds(0, NY)])
        if i < Q:
            rhs = b[:, q * W : (q + 1) * W]
        else:
            rhs = mfull[i - Q, c].reshape(a.shape[1], W)
        rows = part.shape[2]
        for d in (1, 2, 3, 0):
            p = x_peer(d)
            left = a[pl.ds(pl.multiple_of(p * rows, rows), rows), :]
            part[i, p] = dot(left, rhs).astype(BF16)
            if d:
                push(i, 0, part.at[i, p], xrecv.at[i, d - 1], at_x(d))

    def s2(i):
        arrived(i, 0, xrecv.at[i])
        total = part[i, c].astype(F32)
        for d in range(NX - 1):
            total = total + xrecv[i, d].astype(F32)
        mix[i, c] = total.astype(BF16)
        for d in (1, 2, 3):
            push(i, 1, mix.at[i, c], mix.at[i, c], at_x(d))

    def s3(i):
        arrived(i, 1, mix.at[i, pl.ds(0, NX - 1)])
        right = mix[i].reshape(a.shape[0], W)
        left = at[pl.ds(pl.multiple_of((1 - core) * half, half), half), :]
        csend[i] = (dot(left, right) * inv_count).astype(BF16)
        push(i, 2, csend.at[i], crecv.at[i], at_core)
        left = at[pl.ds(pl.multiple_of(core * half, half), half), :]
        chalf[i] = dot(left, right) * inv_count

    def s4(i):
        arrived(i, 2, crecv.at[i])
        ybuf[i] = (chalf[i] + crecv[i].astype(F32)).astype(BF16).reshape(NY, piece, W)
        for d in (1, 2, 3):
            push(i, 3, ybuf.at[i, y_peer(d)], yrecv.at[i, d - 1], at_y(d))

    def s5(i):
        arrived(i, 3, yrecv.at[i])
        total = ybuf[i, y].astype(F32)
        for d in range(NY - 1):
            total = total + yrecv[i, d].astype(F32)
        zbuf[i, : NZ - 1] = total.astype(BF16).reshape(NZ - 1, 16, W)
        zbuf[i, NZ - 1] = jnp.zeros((16, W), BF16)
        for d in range(1, NZ):
            push(i, 4, zbuf.at[i, z_peer(d)], zrecv.at[i, d - 1], at_z(d))

    def s6(i):
        arrived(i, 4, zrecv.at[i])
        total = zbuf[i, z].astype(F32)
        for d in range(NZ - 1):
            total = total + zrecv[i, d].astype(F32)
        if i >= Q:
            q = i - Q
            raw[q] = total.astype(BF16)
            total = jnp.zeros((16, W), F32)
            for k in range(q + 1):
                total = total + dot(raw[k], fbf[q, k])
        zg[i, pl.ds(pl.multiple_of(z * 16, 16), 16), :] = total.astype(BF16)
        mine = zg.at[i, pl.ds(pl.multiple_of(z * 16, 16), 16), :]
        for d in range(1, NZ):
            push(i, 5, mine, mine, at_z(d))

    def s7(i):
        arrived(i, 5, zg.at[i, pl.ds(0, piece), :])
        src = zg.at[i, pl.ds(0, piece), :]
        dst = mfull.at[i, c, core * NY + y]
        for d in (1, 2, 3):
            push(i, 6, src, dst, at_y(d))
        for d in (1, 2, 3):
            push(i, 7, src, dst, at_x(d))
        mfull[i, c, core * NY + y] = zg[i, :piece, :]

    def s8a(i):
        arrived(i, 6, mfull.at[i, 0, pl.ds(0, NY - 1)])
        mine = mfull.at[i, c, pl.ds(core * NY, NY)]
        push(i, 8, mine, mine, at_core)

    def s8b(i):
        arrived(i, 7, mfull.at[i, 0, pl.ds(0, NX - 1)])
        for e in (1, 2, 3):
            held = mfull.at[i, x_peer(e), core * NY + y]
            for d in (1, 2, 3):
                push(i, 9, held, held, at_y(d))

    def s9b(i):
        arrived(i, 9, mfull.at[i, pl.ds(0, NX - 1), pl.ds(0, NY - 1)])
        for e in (1, 2, 3):
            held = mfull.at[i, x_peer(e), pl.ds(core * NY, NY)]
            push(i, 10, held, held, at_core)

    quarter = a.shape[1]

    def factor(i):
        sweep, q = divmod(i, Q)
        lo = q * W
        if sweep:
            arrived(i, 8, mfull.at[i, 0, pl.ds(0, NY)])
        arrived(i, 10, mfull.at[i, pl.ds(0, NX - 1), pl.ds(0, NY)])
        for x in range(NX):
            mt[sweep, pl.ds(lo, W), pl.ds(x * quarter, quarter)] = mfull[i, x].reshape(quarter, W).T
        gram = dot(mt[sweep, : lo + W, :], mfull[i].reshape(NX * quarter, W))
        if sweep:
            wbuf[:, pl.ds(lo, W)] = dot(grad[...], mfull[i].reshape(NX * quarter, W))
        yield
        block = gram[lo:, :]
        if q:
            known = linv[sweep, :lo, :lo]
            upper = dot32(known, gram[:lo, :])
            block = block - dot32(upper, upper, ((0,), (0,)))
            cross = dot32(upper, known, ((0,), (0,)))
        inverse = yield from inverse_factor(block)
        linv[sweep, pl.ds(lo, W), pl.ds(lo, W)] = inverse
        if q:
            low = -dot32(inverse, cross)
            linv[sweep, pl.ds(lo, W), pl.ds(0, lo)] = low
        if q < Q - 1:
            linv[sweep, pl.ds(lo, W), pl.ds(lo + W, Q * W - lo - W)] = jnp.zeros((W, Q * W - lo - W), F32)
        if sweep == 0:
            for k in range(q):
                fbf[q, k] = low[:, k * W : (k + 1) * W].T.astype(BF16)
            fbf[q, q] = inverse.T.astype(BF16)

    def finish():
        inverse = linv[1]
        coefficients = dot32(wbuf[...], inverse, ((1,), (1,)))
        solved = dot32(coefficients, inverse)
        high = solved.astype(BF16)
        low = (solved - high.astype(F32)).astype(BF16)
        for x in range(NX):
            lanes = pl.ds(x * quarter, quarter)
            removed = dot(high, mt[1, :, lanes]) + dot(low, mt[1, :, lanes])
            out[:, lanes] = (grad[:, lanes].astype(F32) - removed).astype(BF16)

    def transpose():
        for k in range(a.shape[0] // W):
            at[:, k * W : (k + 1) * W] = a[k * W : (k + 1) * W, :].T

    stages = (s1, s2, s3, s4, s5, s6, s7, s8a, s8b, s9b)
    factors = [factor(i) for i in range(2 * Q)]
    for task, i in ORDER:
        if task == "T":
            transpose()
        elif task == "F":
            next(factors[i], None)
        else:
            stages[task](i)
    finish()
    for i, stage, like in sent:
        pltpu.make_async_copy(like, like, send.at[i, stage]).wait()


def on_device(activations, start_basis, gradient):
    gradient = gradient.T
    tokens, quarter = activations.shape
    inv_count = 1.0 / (tokens * lax.axis_size("seq"))
    n = 2 * Q
    half = quarter // NC
    piece = half // NY
    rows = tokens // NX
    vmem = pltpu.VMEM
    features = NX * quarter
    return pl.pallas_call(
        functools.partial(kernel, inv_count),
        out_shape=jax.ShapeDtypeStruct(gradient.shape, BF16),
        in_specs=[pl.BlockSpec(memory_space=pltpu.VMEM)] * 3,
        out_specs=pl.BlockSpec(memory_space=pltpu.VMEM),
        scratch_shapes=[
            vmem((quarter, tokens), BF16),
            vmem((n, NX, rows, W), BF16),
            vmem((n, NX - 1, rows, W), BF16),
            vmem((n, NX, rows, W), BF16),
            vmem((n, half, W), BF16),
            vmem((n, half, W), F32),
            vmem((n, half, W), BF16),
            vmem((n, NY, piece, W), BF16),
            vmem((n, NY - 1, piece, W), BF16),
            vmem((n, NZ, 16, W), BF16),
            vmem((n, NZ - 1, 16, W), BF16),
            vmem((n, NZ * 16, W), BF16),
            vmem((n, NX, NC * NY, piece, W), BF16),
            vmem((Q, 16, W), BF16),
            vmem((2, Q * W, features), BF16),
            vmem((2, Q * W, Q * W), F32),
            vmem((Q, Q, W, W), BF16),
            vmem((gradient.shape[0], Q * W), F32),
            pltpu.SemaphoreType.DMA((n, STAGES)),
            pltpu.SemaphoreType.DMA((n, STAGES)),
        ],
        compiler_params=pltpu.CompilerParams(
            collective_id=0, has_side_effects=True, vmem_limit_bytes=60 * 1024 * 1024
        ),
    )(activations, start_basis, gradient).T


def solution(mesh):
    return jax.shard_map(
        on_device,
        mesh=mesh,
        in_specs=(P("seq", "col"), P("col", None), P(None, ("seq", "col"))),
        out_specs=P(None, ("seq", "col")),
        check_vma=False,
    )
```

```python
import functools

import jax
import jax.numpy as jnp
from jax import lax
from jax.experimental import pallas as pl
from jax.experimental.pallas import tpu as pltpu
from jax.sharding import PartitionSpec as P

MESH = pl.DeviceIdType.MESH
F32 = jnp.float32
BF16 = jnp.bfloat16
NX, NY, NZ, NC = 4, 4, 8, 2
Q = 4
W = 128
STAGES = 13
ORDER = (
    (0, 1), (0, 0), (0, 2), (10, 0), (10, 1), (0, 3), (10, 2), (1, 0),
    (1, 1), (10, 3), ("T", 0), (11, 0), (11, 1), (1, 2), (1, 3), (2, 0),
    (2, 1), (3, 0), (11, 2), (3, 1), (11, 3), (4, 0), (2, 2), (4, 1),
    (2, 3), (3, 2), (5, 0), (3, 3), (5, 1), (4, 2), (6, 0), (4, 3),
    (6, 1), (5, 2), (7, 0), (8, 0), (5, 3), (7, 1), (0, 4), (6, 2),
    (0, 5), (6, 3), (8, 1), (10, 4), (9, 0), (7, 2), (8, 2), (10, 5),
    (7, 3), (0, 6), ("F", 0), ("F", 0), (1, 5), ("F", 0), (1, 4), (9, 1),
    (0, 7), ("F", 0), (10, 6), ("F", 0), (11, 4), (11, 5), (8, 3), (9, 2),
    ("F", 1), (2, 4), (1, 6), ("F", 1), (2, 5), ("F", 1), (3, 4), (10, 7),
    ("F", 1), (3, 5), ("F", 1), (1, 7), (4, 4), ("F", 2), (4, 5), (11, 6),
    ("F", 2), (11, 7), (5, 4), (2, 6), ("F", 2), (2, 7), (9, 3), ("F", 2),
    (5, 5), (6, 4), (3, 6), ("F", 2), ("F", 3), (8, 4), (7, 4), (4, 6),
    (3, 7), ("F", 3), ("F", 3), ("F", 3), (6, 5), (9, 4), (5, 6), (4, 7),
    ("F", 3), (8, 5), ("F", 4), (5, 7), ("F", 4), (7, 5), (6, 6), ("F", 4),
    (6, 7), ("F", 4), (8, 6), (9, 5), ("F", 4), (8, 7), ("F", 5), (7, 6),
    ("F", 5), (9, 6), ("F", 5), ("F", 5), ("F", 5), ("F", 6), ("F", 6), ("F", 6),
    (9, 7), ("F", 6), (7, 7), ("F", 6), ("F", 7), ("F", 7), ("F", 7), ("F", 7),
    ("F", 7),
)


def dot(left, right):
    return jnp.dot(left, right, preferred_element_type=F32)


def dot32(left, right, dims=((1,), (0,))):
    return lax.dot_general(
        left, right, (dims, ((), ())), precision=lax.Precision.HIGHEST, preferred_element_type=F32
    )


def across(block, lane):
    return jnp.broadcast_to(block[:, lane : lane + 1], (8, 128))


def reciprocal(value):
    guess = pl.reciprocal(value, approx=True)
    return guess * (2.0 - value * guess)


def eliminate(groups, off):
    sub = lax.broadcasted_iota(jnp.int32, (8, 128), 0)
    groups = list(groups)
    count = len(groups)
    out = []
    for g in range(count):
        if g == count // 2:
            yield
        lo = off + 8 * g
        rows = [jnp.broadcast_to(groups[g][k : k + 1, :], (8, 128)) for k in range(8)]
        square = {(k, c): across(rows[k], lo + c) for k in range(8) for c in range(k, 8)}
        inverse, factor = [], {}
        for k in range(8):
            inverse.append(reciprocal(square[k, k]))
            for i in range(k + 1, 8):
                factor[i, k] = square[k, i] * inverse[k]
                for j in range(i, 8):
                    square[i, j] = square[i, j] - factor[i, k] * square[k, j]
                rows[i] = rows[i] - factor[i, k] * rows[k]
        if g + 1 < count:
            columns = [across(groups[g + 1], lo + k) for k in range(8)]
            for i in range(8):
                for k in range(i):
                    columns[i] = columns[i] - factor[i, k] * columns[k]
            for k in range(8):
                groups[g + 1] = groups[g + 1] - (columns[k] * inverse[k]) * rows[k]
        result = rows[0] * lax.rsqrt(square[0, 0])
        for k in range(1, 8):
            result = jnp.where(sub == k, rows[k] * lax.rsqrt(square[k, k]), result)
        if g + 2 < count:
            turned = result.T
            scaled = [rows[k] * lax.rsqrt(square[k, k]) for k in range(8)]
            for other in range(g + 2, count):
                columns = turned[off + 8 * other : off + 8 * other + 8, :]
                for k in range(8):
                    groups[other] = groups[other] - across(columns, k) * scaled[k]
        out.append(result)
    return jnp.concatenate(out, axis=0)


def inverse_factor(block):
    lane = lax.broadcasted_iota(jnp.int32, (64, 128), 1)
    row = lax.broadcasted_iota(jnp.int32, (64, 128), 0)
    top, bottom = block[:64, :], block[64:, :]
    start = jnp.where(lane < 64, top, jnp.where(lane - 64 == row, 1.0, 0.0))
    first = yield from eliminate([start[8 * g : 8 * g + 8] for g in range(8)], 0)
    first = jnp.where(lane < 64, pltpu.roll(first, 64, 1), 0.0)
    yield
    inv1 = first[:, :64]
    upper = dot32(inv1, top)
    both = dot32(upper, upper, ((0,), (0,)))
    rest = bottom - both[64:, :]
    start = jnp.where(lane >= 64, rest, jnp.where(lane == row, 1.0, 0.0))
    cross = dot32(upper, first, ((0,), (0,)))[64:, :]
    second = yield from eliminate([start[8 * g : 8 * g + 8] for g in range(8)], 64)
    second = jnp.where(lane < 64, second, 0.0)
    low = dot32(second[:, :64], cross)
    last = jnp.where(lane < 64, -low, pltpu.roll(second, 64, 1))
    return jnp.concatenate([first, last], axis=0)


def kernel(inv_count, a, b, grad, out, at, part, xhalf, xsum, xrecv, mix, csend, chalf, crecv, ybuf, yrecv,
           zbuf, zrecv, zg, mfull, raw, mt, linv, fbf, wbuf, send, recv):
    seq, c = lax.axis_index("seq"), lax.axis_index("col")
    core, z, y = lax.rem(seq, NC), lax.rem(seq // NC, NZ), seq // (NC * NZ)

    def x_peer(d):
        return lax.rem(c + d, NX)

    def y_peer(d):
        return lax.rem(y + d, NY)

    def z_peer(d):
        return lax.rem(z + d, NZ)

    def at_x(d):
        return (seq, x_peer(d))

    def at_y(d):
        return ((y_peer(d) * NZ + z) * NC + core, c)

    def at_z(d):
        return ((y * NZ + z_peer(d)) * NC + core, c)

    at_core = ((y * NZ + z) * NC + 1 - core, c)

    barrier = pltpu.get_barrier_semaphore()
    peers = ([at_x(d) for d in range(1, NX)] + [at_y(d) for d in range(1, NY)]
             + [at_z(d) for d in range(1, NZ)] + [at_core])
    for peer in peers:
        pl.semaphore_signal(barrier, inc=1, device_id=peer, device_id_type=MESH)
    pl.semaphore_wait(barrier, len(peers))

    sent = []

    def push(i, stage, src, dst, device):
        copy = pltpu.make_async_remote_copy(
            src_ref=src, dst_ref=dst, send_sem=send.at[i, stage], recv_sem=recv.at[i, stage],
            device_id=device, device_id_type=MESH)
        copy.start()

    def arrived(i, stage, like):
        pltpu.make_async_copy(like, like, recv.at[i, stage]).wait()
        sent.append((i, stage, like))

    half = a.shape[1] // NC
    piece = half // NY

    rows = part.shape[2]
    first, second = pl.ds(0, rows // 2), pl.ds(rows // 2, rows // 2)

    def s1(i):
        q = i % Q
        if i >= Q:
            arrived(i - Q, 8, mfull.at[i - Q, 0, pl.ds(0, NY)])
        if i < Q:
            rhs = b[:, q * W : (q + 1) * W]
        else:
            rhs = mfull[i - Q, c].reshape(a.shape[1], W)
        def multiply(p):
            left = a[pl.ds(pl.multiple_of(p * rows, rows), rows), :]
            part[i, p] = dot(left, rhs).astype(BF16)

        far, right, left = x_peer(2), x_peer(1), x_peer(3)
        multiply(far)
        push(i, 0, part.at[i, far, first], xhalf.at[i, 0], at_x(1))
        push(i, 0, part.at[i, far, second], xhalf.at[i, 1], at_x(3))
        multiply(right)
        push(i, 11, part.at[i, right, second], xrecv.at[i, 0, second], at_x(1))
        multiply(left)
        push(i, 11, part.at[i, left, first], xrecv.at[i, 1, first], at_x(3))
        multiply(c)

    def s1b(i):
        arrived(i, 0, xhalf.at[i])
        for k, (d, part_rows) in enumerate(((1, first), (3, second))):
            xsum[i, k] = (part[i, x_peer(d), part_rows].astype(F32) + xhalf[i, k].astype(F32)).astype(BF16)
            push(i, 11, xsum.at[i, k], xrecv.at[i, k, part_rows], at_x(d))

    def s2(i):
        arrived(i, 11, xrecv.at[i])
        total = part[i, c].astype(F32) + xrecv[i, 0].astype(F32) + xrecv[i, 1].astype(F32)
        mix[i, c] = total.astype(BF16)
        for d in (1, 3):
            push(i, 1, mix.at[i, c], mix.at[i, c], at_x(d))

    def s2b(i):
        arrived(i, 1, mix.at[i, pl.ds(0, 2)])
        for d, part_rows in ((1, first), (3, second)):
            held = mix.at[i, x_peer(NX - d), part_rows]
            push(i, 12, held, held, at_x(d))

    def s3(i):
        arrived(i, 12, mix.at[i, 0])
        right = mix[i].reshape(a.shape[0], W)
        left = at[pl.ds(pl.multiple_of((1 - core) * half, half), half), :]
        csend[i] = (dot(left, right) * inv_count).astype(BF16)
        push(i, 2, csend.at[i], crecv.at[i], at_core)
        left = at[pl.ds(pl.multiple_of(core * half, half), half), :]
        chalf[i] = dot(left, right) * inv_count

    def s4(i):
        arrived(i, 2, crecv.at[i])
        ybuf[i] = (chalf[i] + crecv[i].astype(F32)).astype(BF16).reshape(NY, piece, W)
        for d in (1, 2, 3):
            push(i, 3, ybuf.at[i, y_peer(d)], yrecv.at[i, d - 1], at_y(d))

    def s5(i):
        arrived(i, 3, yrecv.at[i])
        total = ybuf[i, y].astype(F32)
        for d in range(NY - 1):
            total = total + yrecv[i, d].astype(F32)
        zbuf[i, : NZ - 1] = total.astype(BF16).reshape(NZ - 1, 16, W)
        zbuf[i, NZ - 1] = jnp.zeros((16, W), BF16)
        for d in range(1, NZ):
            push(i, 4, zbuf.at[i, z_peer(d)], zrecv.at[i, d - 1], at_z(d))

    def s6(i):
        arrived(i, 4, zrecv.at[i])
        total = zbuf[i, z].astype(F32)
        for d in range(NZ - 1):
            total = total + zrecv[i, d].astype(F32)
        if i >= Q:
            q = i - Q
            raw[q] = total.astype(BF16)
            total = jnp.zeros((16, W), F32)
            for k in range(q + 1):
                total = total + dot(raw[k], fbf[q, k])
        zg[i, pl.ds(pl.multiple_of(z * 16, 16), 16), :] = total.astype(BF16)
        mine = zg.at[i, pl.ds(pl.multiple_of(z * 16, 16), 16), :]
        for d in range(1, NZ):
            push(i, 5, mine, mine, at_z(d))

    def s7(i):
        arrived(i, 5, zg.at[i, pl.ds(0, piece), :])
        src = zg.at[i, pl.ds(0, piece), :]
        dst = mfull.at[i, c, core * NY + y]
        for d in (1, 2, 3):
            push(i, 6, src, dst, at_y(d))
        for d in (1, 2, 3):
            push(i, 7, src, dst, at_x(d))
        mfull[i, c, core * NY + y] = zg[i, :piece, :]

    def s8a(i):
        arrived(i, 6, mfull.at[i, 0, pl.ds(0, NY - 1)])
        mine = mfull.at[i, c, pl.ds(core * NY, NY)]
        push(i, 8, mine, mine, at_core)

    def s8b(i):
        arrived(i, 7, mfull.at[i, 0, pl.ds(0, NX - 1)])
        for e in (1, 2, 3):
            held = mfull.at[i, x_peer(e), core * NY + y]
            for d in (1, 2, 3):
                push(i, 9, held, held, at_y(d))

    def s9b(i):
        arrived(i, 9, mfull.at[i, pl.ds(0, NX - 1), pl.ds(0, NY - 1)])
        for e in (1, 2, 3):
            held = mfull.at[i, x_peer(e), pl.ds(core * NY, NY)]
            push(i, 10, held, held, at_core)

    quarter = a.shape[1]

    def factor(i):
        sweep, q = divmod(i, Q)
        lo = q * W
        if sweep:
            arrived(i, 8, mfull.at[i, 0, pl.ds(0, NY)])
        arrived(i, 10, mfull.at[i, pl.ds(0, NX - 1), pl.ds(0, NY)])
        for x in range(NX):
            mt[sweep, pl.ds(lo, W), pl.ds(x * quarter, quarter)] = mfull[i, x].reshape(quarter, W).T
        gram = dot(mt[sweep, : lo + W, :], mfull[i].reshape(NX * quarter, W))
        if sweep:
            wbuf[:, pl.ds(lo, W)] = dot(grad[...], mfull[i].reshape(NX * quarter, W))
        yield
        block = gram[lo:, :]
        if q:
            known = linv[sweep, :lo, :lo]
            upper = dot32(known, gram[:lo, :])
            block = block - dot32(upper, upper, ((0,), (0,)))
            cross = dot32(upper, known, ((0,), (0,)))
        inverse = yield from inverse_factor(block)
        linv[sweep, pl.ds(lo, W), pl.ds(lo, W)] = inverse
        if q:
            low = -dot32(inverse, cross)
            linv[sweep, pl.ds(lo, W), pl.ds(0, lo)] = low
        if q < Q - 1:
            linv[sweep, pl.ds(lo, W), pl.ds(lo + W, Q * W - lo - W)] = jnp.zeros((W, Q * W - lo - W), F32)
        if sweep == 0:
            for k in range(q):
                fbf[q, k] = low[:, k * W : (k + 1) * W].T.astype(BF16)
            fbf[q, q] = inverse.T.astype(BF16)

    def finish():
        inverse = linv[1]
        coefficients = dot32(wbuf[...], inverse, ((1,), (1,)))
        solved = dot32(coefficients, inverse)
        high = solved.astype(BF16)
        low = (solved - high.astype(F32)).astype(BF16)
        for x in range(NX):
            lanes = pl.ds(x * quarter, quarter)
            removed = dot(high, mt[1, :, lanes]) + dot(low, mt[1, :, lanes])
            out[:, lanes] = (grad[:, lanes].astype(F32) - removed).astype(BF16)

    def transpose():
        for k in range(a.shape[0] // W):
            at[:, k * W : (k + 1) * W] = a[k * W : (k + 1) * W, :].T

    stages = (s1, s2, s3, s4, s5, s6, s7, s8a, s8b, s9b, s1b, s2b)
    factors = [factor(i) for i in range(2 * Q)]
    for task, i in ORDER:
        if task == "T":
            transpose()
        elif task == "F":
            next(factors[i], None)
        else:
            stages[task](i)
    finish()
    for i, stage, like in sent:
        pltpu.make_async_copy(like, like, send.at[i, stage]).wait()


def on_device(activations, start_basis, gradient):
    gradient = gradient.T
    tokens, quarter = activations.shape
    inv_count = 1.0 / (tokens * lax.axis_size("seq"))
    n = 2 * Q
    half = quarter // NC
    piece = half // NY
    rows = tokens // NX
    vmem = pltpu.VMEM
    features = NX * quarter
    return pl.pallas_call(
        functools.partial(kernel, inv_count),
        out_shape=jax.ShapeDtypeStruct(gradient.shape, BF16),
        in_specs=[pl.BlockSpec(memory_space=pltpu.VMEM)] * 3,
        out_specs=pl.BlockSpec(memory_space=pltpu.VMEM),
        scratch_shapes=[
            vmem((quarter, tokens), BF16),
            vmem((n, NX, rows, W), BF16),
            vmem((n, 2, rows // 2, W), BF16),
            vmem((n, 2, rows // 2, W), BF16),
            vmem((n, 2, rows, W), BF16),
            vmem((n, NX, rows, W), BF16),
            vmem((n, half, W), BF16),
            vmem((n, half, W), F32),
            vmem((n, half, W), BF16),
            vmem((n, NY, piece, W), BF16),
            vmem((n, NY - 1, piece, W), BF16),
            vmem((n, NZ, 16, W), BF16),
            vmem((n, NZ - 1, 16, W), BF16),
            vmem((n, NZ * 16, W), BF16),
            vmem((n, NX, NC * NY, piece, W), BF16),
            vmem((Q, 16, W), BF16),
            vmem((2, Q * W, features), BF16),
            vmem((2, Q * W, Q * W), F32),
            vmem((Q, Q, W, W), BF16),
            vmem((gradient.shape[0], Q * W), F32),
            pltpu.SemaphoreType.DMA((n, STAGES)),
            pltpu.SemaphoreType.DMA((n, STAGES)),
        ],
        compiler_params=pltpu.CompilerParams(
            collective_id=0, has_side_effects=True, vmem_limit_bytes=60 * 1024 * 1024
        ),
    )(activations, start_basis, gradient).T


def solution(mesh):
    return jax.shard_map(
        on_device,
        mesh=mesh,
        in_specs=(P("seq", "col"), P("col", None), P(None, ("seq", "col"))),
        out_specs=P(None, ("seq", "col")),
        check_vma=False,
    )
```

```python
import functools

import jax
import jax.numpy as jnp
from jax import lax
from jax.experimental import pallas as pl
from jax.experimental.pallas import tpu as pltpu
from jax.sharding import PartitionSpec as P

MESH = pl.DeviceIdType.MESH
F32 = jnp.float32
BF16 = jnp.bfloat16
NX, NY, NZ, NC = 4, 4, 8, 2
Q = 4
W = 128
STAGES = 13
ORDER = (
    (0, 0), (0, 3), (0, 1), (10, 0), (0, 2), (10, 3), ("T", 0), (10, 1),
    (1, 0), (10, 2), (1, 1), (11, 0), (1, 2), (11, 1), (1, 3), (2, 0),
    (11, 2), (3, 0), (2, 1), (11, 3), (2, 2), (3, 1), (4, 0), (3, 2),
    (2, 3), (4, 1), (5, 0), (4, 2), (3, 3), (5, 1), (6, 0), (5, 2),
    (4, 3), (6, 1), (7, 0), (8, 0), (6, 2), (0, 4), (7, 1), (5, 3),
    (8, 1), (0, 5), (8, 2), (9, 0), (6, 3), (7, 2), (10, 4), (10, 5),
    ("F", 0), ("F", 0), (9, 1), (0, 6), (1, 4), ("F", 0), ("F", 0), (1, 5),
    (10, 6), (7, 3), ("F", 0), ("F", 1), (11, 4), ("F", 1), (11, 5), (1, 6),
    ("F", 1), (0, 7), (2, 4), ("F", 1), (2, 5), (10, 7), (3, 4), ("F", 1),
    (11, 6), (3, 5), (9, 2), (8, 3), (4, 4), (1, 7), (2, 6), (4, 5),
    ("F", 2), (3, 6), (5, 4), (11, 7), ("F", 2), ("F", 2), (5, 5), (2, 7),
    (4, 6), (9, 3), (6, 4), ("F", 2), (3, 7), ("F", 2), (8, 4), (5, 6),
    ("F", 3), ("F", 3), (7, 4), (6, 5), (6, 6), ("F", 3), (4, 7), (9, 4),
    ("F", 3), (8, 5), ("F", 3), (7, 6), (8, 6), (5, 7), ("F", 4), ("F", 4),
    ("F", 4), (7, 5), (6, 7), (9, 5), ("F", 4), ("F", 4), (8, 7), ("F", 5),
    ("F", 5), ("F", 5), (9, 6), ("F", 5), (7, 7), ("F", 5), ("F", 6), (9, 7),
    ("F", 6), ("F", 6), ("F", 6), ("F", 6), ("F", 7), ("F", 7), ("F", 7), ("F", 7),
    ("F", 7),
)


def dot(left, right):
    return jnp.dot(left, right, preferred_element_type=F32)


def dot32(left, right, dims=((1,), (0,))):
    return lax.dot_general(
        left, right, (dims, ((), ())), precision=lax.Precision.HIGHEST, preferred_element_type=F32
    )


def across(block, lane):
    return jnp.broadcast_to(block[:, lane : lane + 1], (8, 128))


def reciprocal(value):
    guess = pl.reciprocal(value, approx=True)
    return guess * (2.0 - value * guess)


def eliminate(groups, off):
    sub = lax.broadcasted_iota(jnp.int32, (8, 128), 0)
    groups = list(groups)
    count = len(groups)
    out = []
    for g in range(count):
        if g == count // 2:
            yield
        lo = off + 8 * g
        rows = [jnp.broadcast_to(groups[g][k : k + 1, :], (8, 128)) for k in range(8)]
        square = {(k, c): across(rows[k], lo + c) for k in range(8) for c in range(k, 8)}
        inverse, factor = [], {}
        for k in range(8):
            inverse.append(reciprocal(square[k, k]))
            for i in range(k + 1, 8):
                factor[i, k] = square[k, i] * inverse[k]
                for j in range(i, 8):
                    square[i, j] = square[i, j] - factor[i, k] * square[k, j]
                rows[i] = rows[i] - factor[i, k] * rows[k]
        if g + 1 < count:
            columns = [across(groups[g + 1], lo + k) for k in range(8)]
            for i in range(8):
                for k in range(i):
                    columns[i] = columns[i] - factor[i, k] * columns[k]
            for k in range(8):
                groups[g + 1] = groups[g + 1] - (columns[k] * inverse[k]) * rows[k]
        result = rows[0] * lax.rsqrt(square[0, 0])
        for k in range(1, 8):
            result = jnp.where(sub == k, rows[k] * lax.rsqrt(square[k, k]), result)
        if g + 2 < count:
            turned = result.T
            scaled = [rows[k] * lax.rsqrt(square[k, k]) for k in range(8)]
            for other in range(g + 2, count):
                columns = turned[off + 8 * other : off + 8 * other + 8, :]
                for k in range(8):
                    groups[other] = groups[other] - across(columns, k) * scaled[k]
        out.append(result)
    return jnp.concatenate(out, axis=0)


def inverse_factor(block):
    lane = lax.broadcasted_iota(jnp.int32, (64, 128), 1)
    row = lax.broadcasted_iota(jnp.int32, (64, 128), 0)
    top, bottom = block[:64, :], block[64:, :]
    start = jnp.where(lane < 64, top, jnp.where(lane - 64 == row, 1.0, 0.0))
    first = yield from eliminate([start[8 * g : 8 * g + 8] for g in range(8)], 0)
    first = jnp.where(lane < 64, pltpu.roll(first, 64, 1), 0.0)
    yield
    inv1 = first[:, :64]
    upper = dot32(inv1, top)
    both = dot32(upper, upper, ((0,), (0,)))
    rest = bottom - both[64:, :]
    start = jnp.where(lane >= 64, rest, jnp.where(lane == row, 1.0, 0.0))
    cross = dot32(upper, first, ((0,), (0,)))[64:, :]
    second = yield from eliminate([start[8 * g : 8 * g + 8] for g in range(8)], 64)
    second = jnp.where(lane < 64, second, 0.0)
    low = dot32(second[:, :64], cross)
    last = jnp.where(lane < 64, -low, pltpu.roll(second, 64, 1))
    return jnp.concatenate([first, last], axis=0)


def kernel(inv_count, a, b, grad, out, at, part, xhalf, xsum, xrecv, mix, csend, chalf, crecv, ybuf, yrecv,
           zbuf, zrecv, zg, mfull, raw, mt, linv, fbf, wbuf, send, recv):
    seq, c = lax.axis_index("seq"), lax.axis_index("col")
    core, z, y = lax.rem(seq, NC), lax.rem(seq // NC, NZ), seq // (NC * NZ)

    def x_peer(d):
        return lax.rem(c + d, NX)

    def y_peer(d):
        return lax.rem(y + d, NY)

    def z_peer(d):
        return lax.rem(z + d, NZ)

    def at_x(d):
        return (seq, x_peer(d))

    def at_y(d):
        return ((y_peer(d) * NZ + z) * NC + core, c)

    def at_z(d):
        return ((y * NZ + z_peer(d)) * NC + core, c)

    at_core = ((y * NZ + z) * NC + 1 - core, c)

    barrier = pltpu.get_barrier_semaphore()
    peers = ([at_x(d) for d in range(1, NX)] + [at_y(d) for d in range(1, NY)]
             + [at_z(d) for d in range(1, NZ)] + [at_core])
    for peer in peers:
        pl.semaphore_signal(barrier, inc=1, device_id=peer, device_id_type=MESH)
    pl.semaphore_wait(barrier, len(peers))

    sent = []

    def push(i, stage, src, dst, device):
        copy = pltpu.make_async_remote_copy(
            src_ref=src, dst_ref=dst, send_sem=send.at[i, stage], recv_sem=recv.at[i, stage],
            device_id=device, device_id_type=MESH)
        copy.start()

    def arrived(i, stage, like):
        pltpu.make_async_copy(like, like, recv.at[i, stage]).wait()
        sent.append((i, stage, like))

    half = a.shape[1] // NC
    piece = half // NY

    rows = part.shape[2]
    first, second = pl.ds(0, rows // 2), pl.ds(rows // 2, rows // 2)

    def s1(i):
        q = i % Q
        if i >= Q:
            arrived(i - Q, 8, mfull.at[i - Q, 0, pl.ds(0, NY)])
        if i < Q:
            rhs = b[:, q * W : (q + 1) * W]
        else:
            rhs = mfull[i - Q, c].reshape(a.shape[1], W)
        def multiply(p):
            left = a[pl.ds(pl.multiple_of(p * rows, rows), rows), :]
            part[i, p] = dot(left, rhs).astype(BF16)

        far, right, left = x_peer(2), x_peer(1), x_peer(3)
        multiply(far)
        push(i, 0, part.at[i, far, first], xhalf.at[i, 0], at_x(1))
        push(i, 0, part.at[i, far, second], xhalf.at[i, 1], at_x(3))
        multiply(right)
        push(i, 11, part.at[i, right, second], xrecv.at[i, 0, second], at_x(1))
        multiply(left)
        push(i, 11, part.at[i, left, first], xrecv.at[i, 1, first], at_x(3))
        multiply(c)

    def s1b(i):
        arrived(i, 0, xhalf.at[i])
        for k, (d, part_rows) in enumerate(((1, first), (3, second))):
            xsum[i, k] = (part[i, x_peer(d), part_rows].astype(F32) + xhalf[i, k].astype(F32)).astype(BF16)
            push(i, 11, xsum.at[i, k], xrecv.at[i, k, part_rows], at_x(d))

    def s2(i):
        arrived(i, 11, xrecv.at[i])
        total = part[i, c].astype(F32) + xrecv[i, 0].astype(F32) + xrecv[i, 1].astype(F32)
        mix[i, c] = total.astype(BF16)
        for d in (1, 3):
            push(i, 1, mix.at[i, c], mix.at[i, c], at_x(d))

    def s2b(i):
        arrived(i, 1, mix.at[i, pl.ds(0, 2)])
        for d, part_rows in ((1, first), (3, second)):
            held = mix.at[i, x_peer(NX - d), part_rows]
            push(i, 12, held, held, at_x(d))

    def s3(i):
        arrived(i, 12, mix.at[i, 0])
        right = mix[i].reshape(a.shape[0], W)
        left = at[pl.ds(pl.multiple_of((1 - core) * half, half), half), :]
        csend[i] = (dot(left, right) * inv_count).astype(BF16)
        push(i, 2, csend.at[i], crecv.at[i], at_core)
        left = at[pl.ds(pl.multiple_of(core * half, half), half), :]
        chalf[i] = dot(left, right) * inv_count

    def s4(i):
        arrived(i, 2, crecv.at[i])
        ybuf[i] = (chalf[i] + crecv[i].astype(F32)).astype(BF16).reshape(NY, piece, W)
        for d in (1, 2, 3):
            push(i, 3, ybuf.at[i, y_peer(d)], yrecv.at[i, d - 1], at_y(d))

    def s5(i):
        arrived(i, 3, yrecv.at[i])
        total = ybuf[i, y].astype(F32)
        for d in range(NY - 1):
            total = total + yrecv[i, d].astype(F32)
        zbuf[i, : NZ - 1] = total.astype(BF16).reshape(NZ - 1, 16, W)
        zbuf[i, NZ - 1] = jnp.zeros((16, W), BF16)
        for d in range(1, NZ):
            push(i, 4, zbuf.at[i, z_peer(d)], zrecv.at[i, d - 1], at_z(d))

    def s6(i):
        arrived(i, 4, zrecv.at[i])
        total = zbuf[i, z].astype(F32)
        for d in range(NZ - 1):
            total = total + zrecv[i, d].astype(F32)
        if i >= Q:
            q = i - Q
            raw[q] = total.astype(BF16)
            total = jnp.zeros((16, W), F32)
            for k in range(q + 1):
                total = total + dot(raw[k], fbf[q, k])
        zg[i, pl.ds(pl.multiple_of(z * 16, 16), 16), :] = total.astype(BF16)
        mine = zg.at[i, pl.ds(pl.multiple_of(z * 16, 16), 16), :]
        for d in range(1, NZ):
            push(i, 5, mine, mine, at_z(d))

    def s7(i):
        arrived(i, 5, zg.at[i, pl.ds(0, piece), :])
        src = zg.at[i, pl.ds(0, piece), :]
        dst = mfull.at[i, c, core * NY + y]
        for d in (1, 2, 3):
            push(i, 6, src, dst, at_y(d))
        for d in (1, 2, 3):
            push(i, 7, src, dst, at_x(d))
        mfull[i, c, core * NY + y] = zg[i, :piece, :]

    def s8a(i):
        arrived(i, 6, mfull.at[i, 0, pl.ds(0, NY - 1)])
        mine = mfull.at[i, c, pl.ds(core * NY, NY)]
        push(i, 8, mine, mine, at_core)

    def s8b(i):
        arrived(i, 7, mfull.at[i, 0, pl.ds(0, NX - 1)])
        for e in (1, 2, 3):
            held = mfull.at[i, x_peer(e), core * NY + y]
            for d in (1, 2, 3):
                push(i, 9, held, held, at_y(d))

    def s9b(i):
        arrived(i, 9, mfull.at[i, pl.ds(0, NX - 1), pl.ds(0, NY - 1)])
        for e in (1, 2, 3):
            held = mfull.at[i, x_peer(e), pl.ds(core * NY, NY)]
            push(i, 10, held, held, at_core)

    quarter = a.shape[1]

    def factor(i):
        sweep, q = divmod(i, Q)
        lo = q * W
        if sweep:
            arrived(i, 8, mfull.at[i, 0, pl.ds(0, NY)])
        arrived(i, 10, mfull.at[i, pl.ds(0, NX - 1), pl.ds(0, NY)])
        for x in range(NX):
            mt[sweep, pl.ds(lo, W), pl.ds(x * quarter, quarter)] = mfull[i, x].reshape(quarter, W).T
        gram = dot(mt[sweep, : lo + W, :], mfull[i].reshape(NX * quarter, W))
        if sweep:
            wbuf[:, pl.ds(lo, W)] = dot(grad[...], mfull[i].reshape(NX * quarter, W))
        yield
        block = gram[lo:, :]
        if q:
            known = linv[sweep, :lo, :lo]
            upper = dot32(known, gram[:lo, :])
            block = block - dot32(upper, upper, ((0,), (0,)))
            cross = dot32(upper, known, ((0,), (0,)))
        inverse = yield from inverse_factor(block)
        linv[sweep, pl.ds(lo, W), pl.ds(lo, W)] = inverse
        if q:
            low = -dot32(inverse, cross)
            linv[sweep, pl.ds(lo, W), pl.ds(0, lo)] = low
        if q < Q - 1:
            linv[sweep, pl.ds(lo, W), pl.ds(lo + W, Q * W - lo - W)] = jnp.zeros((W, Q * W - lo - W), F32)
        if sweep == 0:
            for k in range(q):
                fbf[q, k] = low[:, k * W : (k + 1) * W].T.astype(BF16)
            fbf[q, q] = inverse.T.astype(BF16)

    def finish():
        inverse = linv[1]
        coefficients = dot32(wbuf[...], inverse, ((1,), (1,)))
        solved = dot32(coefficients, inverse)
        high = solved.astype(BF16)
        low = (solved - high.astype(F32)).astype(BF16)
        for x in range(NX):
            lanes = pl.ds(x * quarter, quarter)
            removed = dot(high, mt[1, :, lanes]) + dot(low, mt[1, :, lanes])
            out[:, lanes] = (grad[:, lanes].astype(F32) - removed).astype(BF16)

    def transpose():
        for k in range(a.shape[0] // W):
            at[:, k * W : (k + 1) * W] = a[k * W : (k + 1) * W, :].T

    stages = (s1, s2, s3, s4, s5, s6, s7, s8a, s8b, s9b, s1b, s2b)
    factors = [factor(i) for i in range(2 * Q)]
    for task, i in ORDER:
        if task == "T":
            transpose()
        elif task == "F":
            next(factors[i], None)
        else:
            stages[task](i)
    finish()
    for i, stage, like in sent:
        pltpu.make_async_copy(like, like, send.at[i, stage]).wait()


def on_device(activations, start_basis, gradient):
    gradient = gradient.T
    tokens, quarter = activations.shape
    inv_count = 1.0 / (tokens * lax.axis_size("seq"))
    n = 2 * Q
    half = quarter // NC
    piece = half // NY
    rows = tokens // NX
    vmem = pltpu.VMEM
    features = NX * quarter
    return pl.pallas_call(
        functools.partial(kernel, inv_count),
        out_shape=jax.ShapeDtypeStruct(gradient.shape, BF16),
        in_specs=[pl.BlockSpec(memory_space=pltpu.VMEM)] * 3,
        out_specs=pl.BlockSpec(memory_space=pltpu.VMEM),
        scratch_shapes=[
            vmem((quarter, tokens), BF16),
            vmem((n, NX, rows, W), BF16),
            vmem((n, 2, rows // 2, W), BF16),
            vmem((n, 2, rows // 2, W), BF16),
            vmem((n, 2, rows, W), BF16),
            vmem((n, NX, rows, W), BF16),
            vmem((n, half, W), BF16),
            vmem((n, half, W), F32),
            vmem((n, half, W), BF16),
            vmem((n, NY, piece, W), BF16),
            vmem((n, NY - 1, piece, W), BF16),
            vmem((n, NZ, 16, W), BF16),
            vmem((n, NZ - 1, 16, W), BF16),
            vmem((n, NZ * 16, W), BF16),
            vmem((n, NX, NC * NY, piece, W), BF16),
            vmem((Q, 16, W), BF16),
            vmem((2, Q * W, features), BF16),
            vmem((2, Q * W, Q * W), F32),
            vmem((Q, Q, W, W), BF16),
            vmem((gradient.shape[0], Q * W), F32),
            pltpu.SemaphoreType.DMA((n, STAGES)),
            pltpu.SemaphoreType.DMA((n, STAGES)),
        ],
        compiler_params=pltpu.CompilerParams(
            collective_id=0, has_side_effects=True, vmem_limit_bytes=60 * 1024 * 1024
        ),
    )(activations, start_basis, gradient).T


def solution(mesh):
    return jax.shard_map(
        on_device,
        mesh=mesh,
        in_specs=(P("seq", "col"), P("col", None), P(None, ("seq", "col"))),
        out_specs=P(None, ("seq", "col")),
        check_vma=False,
    )
```
